32 devices in a mesh: occ: 4 (over y, core), vir: 8 (over z, x).
Axes of the slice: x: 2, y: 2, z: 4, core: 2. Of those that a mesh axis runs over, the one named last changes fastest.
Arguments:
- amplitudes: bfloat16 [2304, 8192], P('occ', 'vir'), may hold values from -6 to 6
- integrals: bfloat16 [8, 8, 1024, 1024], P('vir'), may hold values from -0.0625 to 0.0625
- cd_tiles: int32 [8, 8], P('vir'), may hold values from 0 to 7, as said below
- cd_count: int32 [8], P('vir'), may hold values from 1 to 8, as said below
Outputs:
- residual: bfloat16 [2304, 8192], P('occ', 'vir')
The draws below stay inside these ranges and needn't reach their ends.
Inputs may be any that keep to these rules, and one draw needn't show every extreme that they name: `cd_tiles`: entries of one row are distinct and the first is the row's own pair tile. `cd_count`: slots at or past the count are unused.
All inputs are finite; a program needn't handle non-finite values.
Results may differ from the reference program's by a relative error of at most 0.0075.
Values may be sent and summed in bfloat16 or wider, within the bound.
A program may use at most 128 MiB of HBM per device.

```python
import jax
import jax.numpy as jnp
from jax import lax

TW = 32
K = 1024
CD_MAX = 8
NO = 48
ROWS = 2304
NPT = 8


def draw_cd_tiles(key, part):
    row_keys = jax.random.split(key, NPT)

    def one_row(row_key, tile_pos):
        shuffled = jax.random.permutation(row_key, NPT - 1).astype(jnp.int32) + 1
        offsets = jnp.concatenate([jnp.zeros((1,), jnp.int32), shuffled[:CD_MAX - 1]])
        return (offsets + tile_pos) % NPT
    return jax.vmap(one_row)(row_keys, jnp.arange(NPT, dtype=jnp.int32)).astype(jnp.int32)


def draw_cd_count(key, part):
    first_key, second_key, third_key, top_key, low_key = jax.random.split(key, 5)
    first = jax.random.randint(first_key, (NPT,), 1, CD_MAX + 1)
    second = jax.random.randint(second_key, (NPT,), 1, CD_MAX + 1)
    third = jax.random.randint(third_key, (NPT,), 1, CD_MAX + 1)
    counted = jnp.maximum(jnp.maximum(first, second), third)
    top_index = jax.random.randint(top_key, (), 0, NPT)
    low_index = (top_index + 1 + jax.random.randint(low_key, (), 0, NPT - 1)) % NPT
    positions = jnp.arange(NPT, dtype=jnp.int32)
    counted = jnp.where(positions == top_index, CD_MAX, counted)
    counted = jnp.where(positions == low_index, 1, counted)
    return counted.astype(jnp.int32)


def steps_of(own_key, dims, cuts, least, top_value):
    level, own = 1.0, jax.random.fold_in(own_key, 6)
    for axis_at, blocks in cuts:
        draws = jnp.exp(jax.random.uniform(jax.random.fold_in(own, axis_at), (blocks,), jnp.float32, least / len(cuts), top_value / len(cuts)))
        level = level * jnp.repeat(draws, dims[axis_at] // blocks).reshape([-1 if axis == axis_at else 1 for axis in range(len(dims))])
    return level


def bell_draw(rng, shape, spread, most, cuts=(), kind=jnp.bfloat16):
    result = spread * jax.random.normal(rng, shape, jnp.float32)
    if cuts:
        result = result * steps_of(rng, shape, cuts, -0.22, 0.18)
    return jnp.clip(result, -most, most).astype(kind)


def setup_inputs(seed: int = 0) -> dict:
    key_of = jax.random.split(jax.random.key(seed), 5)
    return {
        "amplitudes": bell_draw(key_of[0], (ROWS, NPT * K), 1.0, 6.0, ((0, 4), (1, 8))),
        "integrals": bell_draw(key_of[1], (NPT, CD_MAX, K, K), (CD_MAX * K) ** -0.5, 0.0625, ((0, 8),)),
        "cd_tiles": draw_cd_tiles(jax.random.fold_in(key_of[4], 71), 0),
        "cd_count": draw_cd_count(jax.random.fold_in(key_of[4], 71), 0),
    }


def reference(amplitudes, integrals, cd_tiles, cd_count):
    def one_pair_tile(tile_pos):
        listed = cd_tiles[tile_pos]
        live_count = cd_count[tile_pos]
        own_blocks = integrals[tile_pos]

        def add_slot(slot_pos, running):
            tile_id = listed[slot_pos].astype(jnp.int32)

            def apply_block(current):
                columns = lax.dynamic_slice_in_dim(amplitudes, (tile_id * K).astype(jnp.int32), K, 1)
                int_block = lax.dynamic_index_in_dim(own_blocks, slot_pos, 0, keepdims=False)
                return current + lax.dot_general(columns, int_block, (((1,), (1,)), ((), ())), preferred_element_type=jnp.float32)

            return lax.cond(slot_pos < live_count, apply_block, lambda current: current, running)

        zero_block = jnp.zeros((ROWS, K), jnp.float32)
        return lax.fori_loop(0, CD_MAX, add_slot, zero_block).astype(jnp.bfloat16)

    ladder = lax.map(one_pair_tile, jnp.arange(NPT, dtype=jnp.int32))
    ladder = ladder.transpose(1, 0, 2).reshape(NO, NO, NPT // 2, 2, TW, TW)
    mirrored = ladder.transpose(1, 0, 2, 3, 5, 4)[:, :, :, ::-1]
    summed = ladder.astype(jnp.float32) + mirrored.astype(jnp.float32)
    return summed.astype(jnp.bfloat16).reshape(ROWS, NPT * K)
```

```python
import functools
import math

import jax
import jax.numpy as jnp
from jax import lax
from jax.experimental import pallas as pl
from jax.experimental.pallas import tpu as pltpu
from jax.sharding import PartitionSpec as P

VMEM_BYTES = 52 * 2**20
COLS = 256
MESH = pl.DeviceIdType.MESH
X_FIRST = 1


def select(table, at):
    found = jnp.int32(table[0])
    for pos in range(1, len(table)):
        found = jnp.where(at == pos, jnp.int32(table[pos]), found)
    return found


def ladder_kernel(n_occ, n_vir, slot_ref, amp_ref, int_hbm, out_ref,
                  gath, ints, turn, flip, lad, mir, acc,
                  int_sem, send_sem, recv_sem, swap_send, swap_recv):
    n_line = n_vir // 2
    n_blocks, cd_max = n_occ, int_hbm.shape[0]
    rows, k = amp_ref.shape[1:]
    width, side = math.isqrt(k), math.isqrt(rows)
    occ, vir = lax.axis_index("occ"), lax.axis_index("vir")
    line, pair = vir // 2, vir % 2
    partner = line * 2 + 1 - pair

    near = [sorted(range(n_line), key=lambda at: (abs(at - here), at)) for here in range(n_line)]
    by_rank = [select([near[here][rank] for here in range(n_line)], line) for rank in range(n_line)]

    def block_of(step):
        flipped = n_blocks - 1 - step
        out, bit = 0, 1
        while bit < n_blocks:
            out = out + bit * (((occ // bit) % 2 + (flipped // bit) % 2) % 2)
            bit *= 2
        return out

    barrier = pltpu.get_barrier_semaphore()

    @pl.when(line > 0)
    def _():
        pl.semaphore_signal(barrier, inc=1, device_id=(occ, vir - 2), device_id_type=MESH)

    @pl.when(line < n_line - 1)
    def _():
        pl.semaphore_signal(barrier, inc=1, device_id=(occ, vir + 2), device_id_type=MESH)

    for other in range(n_occ):
        pl.semaphore_signal(barrier, inc=1, device_id=(other, partner), device_id_type=MESH)

    fetch = pltpu.make_async_copy(int_hbm, ints.at[pl.ds(0, cd_max)], int_sem)
    fetch.start()
    for step in range(n_blocks):
        gath[step, vir] = amp_ref[block_of(step)]
    waits = n_occ + jnp.where(line > 0, 1, 0) + jnp.where(line < n_line - 1, 1, 0)
    pl.semaphore_wait(barrier, waits)

    def copies(step, at, own_column):
        tile = at * 2 + (pair if own_column else 1 - pair)
        crossed = step == X_FIRST
        up = (at <= line) & (line < n_line - 1)
        down = (at >= line) & (line > 0)
        if own_column:
            across = jnp.logical_not(crossed) | (at == line)
        else:
            up, down, across = up & crossed, down & crossed, None
        plan = [(0, up, vir + 2), (1, down, vir - 2), (2, across, partner)]

        def copy(way, target):
            return pltpu.make_async_remote_copy(
                src_ref=gath.at[step, tile],
                dst_ref=gath.at[step, tile],
                send_sem=send_sem.at[way, step, tile],
                recv_sem=recv_sem.at[step, tile],
                device_id=(occ, target),
                device_id_type=MESH,
            )

        return [(cond, functools.partial(copy, way, target))
                for way, cond, target in plan if cond is not None]

    def forward(step, at, own_column):
        for cond, make in copies(step, at, own_column):
            @pl.when(cond)
            def _(make=make):
                make().start()

    def arrived(step, at, own_column):
        tile = at * 2 + (pair if own_column else 1 - pair)
        pltpu.make_async_remote_copy(
            src_ref=gath.at[step, tile], dst_ref=gath.at[step, tile],
            send_sem=send_sem.at[0, step, tile], recv_sem=recv_sem.at[step, tile],
            device_id=(occ, partner), device_id_type=MESH,
        ).wait_recv()

    def product(step, at, own_column, first):
        tile = at * 2 + (pair if own_column else 1 - pair)
        slot = slot_ref[tile]

        def part(n, carry):
            cols = pl.ds(pl.multiple_of(n * COLS, COLS), COLS)
            term = lax.dot_general(
                gath[step, tile], ints[slot, cols, :], (((1,), (1,)), ((), ())),
                preferred_element_type=jnp.float32)
            if first:
                acc[:, cols] = term
            else:
                acc[:, cols] += term
            return carry

        lax.fori_loop(0, k // COLS, part, 0)

    def swap(step):
        return pltpu.make_async_remote_copy(
            src_ref=lad.at[step], dst_ref=mir.at[step],
            send_sem=swap_send.at[step], recv_sem=swap_recv.at[step],
            device_id=(block_of(step), partner), device_id_type=MESH,
        )

    def finish(step):
        swap(step).wait_recv()
        block = block_of(step)

        def part(n, carry):
            cols = pl.ds(pl.multiple_of(n * COLS, COLS), COLS)
            turned = jnp.dot(mir[step], turn[:, cols], preferred_element_type=jnp.float32)
            mirrored = jnp.dot(flip[...], turned.astype(jnp.bfloat16), preferred_element_type=jnp.float32)
            out_ref[block, :, cols] = (lad[step, :, cols].astype(jnp.float32) + mirrored).astype(out_ref.dtype)
            return carry

        lax.fori_loop(0, k // COLS, part, 0)

    forward(0, line, True)
    ints[cd_max] = jnp.zeros((k, k), jnp.bfloat16)

    def build(n, carry):
        cols = pl.ds(pl.multiple_of(n * COLS, COLS), COLS)
        row = lax.broadcasted_iota(jnp.int32, (k, COLS), 0)
        col = lax.broadcasted_iota(jnp.int32, (k, COLS), 1) + n * COLS
        turn[:, cols] = jnp.where(row == (col % width) * width + col // width, 1.0, 0.0).astype(jnp.bfloat16)
        return carry

    lax.fori_loop(0, k // COLS, build, 0)
    row = lax.broadcasted_iota(jnp.int32, (rows, rows), 0)
    col = lax.broadcasted_iota(jnp.int32, (rows, rows), 1)
    flip[...] = jnp.where(row == (col % side) * side + col // side, 1.0, 0.0).astype(jnp.bfloat16)
    fetch.wait()

    order = [(0, True)]
    for rank in range(1, n_line):
        order += [(rank, True), (rank - 1, False)]
    order.append((n_line - 1, False))

    def visit(step, carry):
        @pl.when(step + 1 < n_blocks)
        def _():
            forward(step + 1, line, True)

        for number, (rank, own_column) in enumerate(order):
            at = by_rank[rank]
            if number:
                arrived(step, at, own_column)
                forward(step, at, own_column)
            product(step, at, own_column, number == 0)
        lad[step] = acc[...].astype(jnp.bfloat16)
        swap(step).start()

        @pl.when(step > 0)
        def _():
            finish(step - 1)

        return carry

    lax.fori_loop(0, n_blocks, visit, 0)
    finish(n_blocks - 1)

    def drain(step, carry):
        for rank, own_column in order:
            for cond, make in copies(step, by_rank[rank], own_column):
                @pl.when(cond)
                def _(make=make):
                    make().wait_send()
        swap(step).wait_send()
        return carry

    lax.fori_loop(0, n_blocks, drain, 0)


def fused(amplitudes, integrals, cd_tiles, cd_count):
    n_occ, n_vir = lax.axis_size("occ"), lax.axis_size("vir")
    rows, k = amplitudes.shape
    cd_max = integrals.shape[1]
    side = math.isqrt(rows // n_occ)
    listed, live = cd_tiles[0], cd_count[0]
    slots = jnp.arange(cd_max, dtype=jnp.int32)
    hit = (listed[None, :] == jnp.arange(n_vir, dtype=jnp.int32)[:, None]) & (slots < live)[None, :]
    slot_of = jnp.min(jnp.where(hit, slots[None, :], cd_max), axis=1).astype(jnp.int32)
    blocks = amplitudes.reshape(side, n_occ, side, k).transpose(1, 0, 2, 3).reshape(n_occ, side * side, k)
    block = side * side
    bf16 = jnp.bfloat16
    result = pl.pallas_call(
        functools.partial(ladder_kernel, n_occ, n_vir),
        out_shape=jax.ShapeDtypeStruct(blocks.shape, bf16),
        in_specs=[
            pl.BlockSpec(memory_space=pltpu.SMEM),
            pl.BlockSpec(memory_space=pltpu.VMEM),
            pl.BlockSpec(memory_space=pl.ANY),
        ],
        out_specs=pl.BlockSpec(memory_space=pltpu.VMEM),
        scratch_shapes=[
            pltpu.VMEM((n_occ, n_vir, block, k), bf16),
            pltpu.VMEM((cd_max + 1, k, k), bf16),
            pltpu.VMEM((k, k), bf16),
            pltpu.VMEM((block, block), bf16),
            pltpu.VMEM((n_occ, block, k), bf16),
            pltpu.VMEM((n_occ, block, k), bf16),
            pltpu.VMEM((block, k), jnp.float32),
            pltpu.SemaphoreType.DMA,
            pltpu.SemaphoreType.DMA((3, n_occ, n_vir)),
            pltpu.SemaphoreType.DMA((n_occ, n_vir)),
            pltpu.SemaphoreType.DMA((n_occ,)),
            pltpu.SemaphoreType.DMA((n_occ,)),
        ],
        compiler_params=pltpu.CompilerParams(
            collective_id=0, has_side_effects=True, vmem_limit_bytes=VMEM_BYTES),
        cost_estimate=pl.CostEstimate(
            flops=2 * rows * k * k * (n_vir + 1), bytes_accessed=2 * cd_max * k * k, transcendentals=0),
    )(slot_of, blocks, integrals[0])
    return result.reshape(n_occ, side, side, k).transpose(1, 0, 2, 3).reshape(rows, k)


def gathered_whole(amplitudes, integrals, cd_tiles, cd_count):
    n_occ = lax.axis_size("occ")
    rows, k = amplitudes.shape
    side, width = math.isqrt(rows // n_occ), math.isqrt(k)
    listed, live, blocks = cd_tiles[0], cd_count[0], integrals[0]
    gathered = lax.all_gather(amplitudes, "vir", axis=1, tiled=True)

    def visit_slot(slot, running):
        def apply_block(current):
            columns = lax.dynamic_slice_in_dim(gathered, listed[slot] * k, k, 1)
            block = lax.dynamic_index_in_dim(blocks, slot, 0, keepdims=False)
            return current + lax.dot_general(
                columns, block, (((1,), (1,)), ((), ())), preferred_element_type=jnp.float32)

        return lax.cond(slot < live, apply_block, lambda current: current, running)

    zero = jnp.zeros((rows, k), jnp.float32)
    ladder = lax.fori_loop(0, blocks.shape[0], visit_slot, zero).astype(jnp.bfloat16)
    swapped = lax.all_to_all(ladder.reshape(side, n_occ, side, k), "occ", split_axis=1, concat_axis=1, tiled=True)
    swapped = swapped.transpose(2, 1, 0, 3).reshape(rows, k)
    swapped = lax.ppermute(swapped, "vir", [(at, at ^ 1) for at in range(lax.axis_size("vir"))])
    mirrored = swapped.reshape(rows, width, width).transpose(0, 2, 1).reshape(rows, k)
    return (ladder.astype(jnp.float32) + mirrored.astype(jnp.float32)).astype(jnp.bfloat16)


def on_device(amplitudes, integrals, cd_tiles, cd_count):
    rows, k = amplitudes.shape
    needed = 2 * (rows * k * (lax.axis_size("vir") + 6) + (integrals.shape[1] + 2) * k * k)
    run = fused if needed < VMEM_BYTES else gathered_whole
    return run(amplitudes, integrals, cd_tiles, cd_count)


def solution(mesh):
    placed = (P("occ", "vir"), P("vir", None, None, None), P("vir", None), P("vir"))
    return jax.shard_map(
        on_device, mesh=mesh, in_specs=placed, out_specs=P("occ", "vir"), check_vma=False
    )
```

```python
import functools
import math

import jax
import jax.numpy as jnp
from jax import lax
from jax.experimental import pallas as pl
from jax.experimental.pallas import tpu as pltpu
from jax.sharding import PartitionSpec as P

VMEM_BYTES = 52 * 2**20
COLS = 256
LAG = 2
EARLY = 4
OWN_LAG = 1
MESH = pl.DeviceIdType.MESH


def select(table, at):
    found = jnp.int32(table[0])
    for pos in range(1, len(table)):
        found = jnp.where(at == pos, jnp.int32(table[pos]), found)
    return found


def ladder_kernel(n_occ, n_vir, slot_ref, amp_ref, int_hbm, out_ref,
                  gath, ints, turn, flip, lad, mir, acc, pick,
                  int_sem, send_sem, recv_sem, swap_send, swap_recv):
    n_line = n_vir // 2
    n_blocks, cd_max = n_occ, int_hbm.shape[0]
    rows, k = lad.shape[1:]
    width, side = math.isqrt(k), math.isqrt(rows)
    occ, vir = lax.axis_index("occ"), lax.axis_index("vir")
    line, pair = vir // 2, vir % 2
    partner = line * 2 + 1 - pair

    near = [sorted(range(n_line), key=lambda at: (abs(at - here), abs(2 * at - n_line + 1))) for here in range(n_line)]
    by_rank = [select([near[here][rank] for here in range(n_line)], line) for rank in range(n_line)]

    def block_of(step):
        flipped = n_blocks - 1 - step
        out, bit = 0, 1
        while bit < n_blocks:
            out = out + bit * (((occ // bit) % 2 + (flipped // bit) % 2) % 2)
            bit *= 2
        return out

    barrier = pltpu.get_barrier_semaphore()

    @pl.when(line > 0)
    def _():
        pl.semaphore_signal(barrier, inc=1, device_id=(occ, vir - 2), device_id_type=MESH)

    @pl.when(line < n_line - 1)
    def _():
        pl.semaphore_signal(barrier, inc=1, device_id=(occ, vir + 2), device_id_type=MESH)

    for other in range(n_occ):
        pl.semaphore_signal(barrier, inc=1, device_id=(other, partner), device_id_type=MESH)

    fetch = pltpu.make_async_copy(int_hbm, ints.at[pl.ds(0, cd_max)], int_sem)
    fetch.start()

    def group(step):
        at = lax.broadcasted_iota(jnp.int32, (rows, n_blocks * rows), 0)
        source = lax.broadcasted_iota(jnp.int32, (rows, n_blocks * rows), 1)
        wanted = (at // side) * (side * n_blocks) + block_of(step) * side + at % side
        pick[...] = jnp.where(source == wanted, 1.0, 0.0).astype(jnp.bfloat16)

        def part(n, carry):
            cols = pl.ds(pl.multiple_of(n * COLS, COLS), COLS)
            gath[step, vir, :, cols] = jnp.dot(
                pick[...], amp_ref[:, cols], preferred_element_type=jnp.float32).astype(jnp.bfloat16)
            return carry

        lax.fori_loop(0, k // COLS, part, 0)

    group(0)
    waits = n_occ + jnp.where(line > 0, 1, 0) + jnp.where(line < n_line - 1, 1, 0)
    pl.semaphore_wait(barrier, waits)

    early = max(16, rows // EARLY // 16 * 16)
    parts = [(0, rows - early), (rows - early, early)]

    def copies(step, at, own_column, part):
        tile = at * 2 + (pair if own_column else 1 - pair)
        up = (at <= line) & (line < n_line - 1)
        down = (at >= line) & (line > 0)
        plan = []
        if own_column or part == 1:
            plan = [(0, up, vir + 2), (1, down, vir - 2)]
        if own_column:
            plan.append((2, at == line if part == 1 else at >= 0, partner))

        def copy(way, target):
            block = gath.at[step, tile, pl.ds(*parts[part])]
            return pltpu.make_async_remote_copy(
                src_ref=block, dst_ref=block,
                send_sem=send_sem.at[way, part, step, tile],
                recv_sem=recv_sem.at[part, step, tile],
                device_id=(occ, target), device_id_type=MESH,
            )

        return [(cond, functools.partial(copy, way, target)) for way, cond, target in plan]

    def forward(step, at, own_column, part):
        for cond, make in reversed(copies(step, at, own_column, part)):
            @pl.when(cond)
            def _(make=make):
                make().start()

    def send_own(step):
        forward(step, line, True, 1)
        forward(step, line, True, 0)

    def arrived(step, at, own_column, part):
        tile = at * 2 + (pair if own_column else 1 - pair)
        block = gath.at[step, tile, pl.ds(*parts[part])]
        pltpu.make_async_remote_copy(
            src_ref=block, dst_ref=block,
            send_sem=send_sem.at[0, part, step, tile], recv_sem=recv_sem.at[part, step, tile],
            device_id=(occ, partner), device_id_type=MESH,
        ).wait_recv()

    def take(step, at, own_column, part):
        arrived(step, at, own_column, part)
        forward(step, at, own_column, part)

    def product(step, at, own_column, first):
        tile = at * 2 + (pair if own_column else 1 - pair)
        slot = slot_ref[tile]

        def part(n, carry):
            cols = pl.ds(pl.multiple_of(n * COLS, COLS), COLS)
            term = lax.dot_general(
                gath[step, tile], ints[slot, cols, :], (((1,), (1,)), ((), ())),
                preferred_element_type=jnp.float32)
            if first:
                acc[step % 2, :, cols] = term
            else:
                acc[step % 2, :, cols] += term
            return carry

        lax.fori_loop(0, k // COLS, part, 0)

    def swap(step):
        return pltpu.make_async_remote_copy(
            src_ref=lad.at[step], dst_ref=mir.at[step],
            send_sem=swap_send.at[step], recv_sem=swap_recv.at[step],
            device_id=(block_of(step), partner), device_id_type=MESH,
        )

    def finish(step):
        swap(step).wait_recv()
        block = block_of(step)

        def part(n, carry):
            cols = pl.ds(pl.multiple_of(n * COLS, COLS), COLS)
            turned = jnp.dot(mir[step], turn[:, cols], preferred_element_type=jnp.float32)
            mirrored = jnp.dot(flip[...], turned.astype(jnp.bfloat16), preferred_element_type=jnp.float32)
            out_ref[block, :, cols] = (lad[step, :, cols].astype(jnp.float32) + mirrored).astype(out_ref.dtype)
            return carry

        lax.fori_loop(0, k // COLS, part, 0)

    def build(n, carry):
        cols = pl.ds(pl.multiple_of(n * COLS, COLS), COLS)
        row = lax.broadcasted_iota(jnp.int32, (k, COLS), 0)
        col = lax.broadcasted_iota(jnp.int32, (k, COLS), 1) + n * COLS
        turn[:, cols] = jnp.where(row == (col % width) * width + col // width, 1.0, 0.0).astype(jnp.bfloat16)
        return carry

    def along(step, rank):
        at = by_rank[rank]
        if rank == 0:
            if step + 1 < n_blocks:
                send_own(step + 1)
        else:
            take(step, at, True, 0)
            take(step, at, True, 1)
        take(step, at, False, 1)

    def own(step, rank):
        if step == 0 and rank == 0:
            ints[cd_max] = jnp.zeros((k, k), jnp.bfloat16)
            fetch.wait()
        product(step, by_rank[rank], True, rank == 0)

    def across(step, rank):
        at = by_rank[rank]
        arrived(step, at, False, 0)
        product(step, at, False, False)
        if rank == n_line - 1:
            lad[step] = acc[step % 2].astype(jnp.bfloat16)
            swap(step).start()

    send_own(0)
    for step in range(1, n_blocks):
        group(step)
    events = [(step, rank) for step in range(n_blocks) for rank in range(n_line)]
    for number in range(len(events) + LAG):
        if number < len(events):
            along(*events[number])
        if 0 <= number - OWN_LAG < len(events):
            own(*events[number - OWN_LAG])
        if number == 2:
            lax.fori_loop(0, k // COLS, build, 0)
            row = lax.broadcasted_iota(jnp.int32, (rows, rows), 0)
            col = lax.broadcasted_iota(jnp.int32, (rows, rows), 1)
            flip[...] = jnp.where(row == (col % side) * side + col // side, 1.0, 0.0).astype(jnp.bfloat16)
        if number >= LAG:
            step, rank = events[number - LAG]
            across(step, rank)
            if step > 0 and rank == n_line - 2:
                finish(step - 1)
    finish(n_blocks - 1)

    def drain(step, carry):
        for rank in range(n_line):
            for own_column, part in ((True, 0), (True, 1), (False, 1)):
                for cond, make in copies(step, by_rank[rank], own_column, part):
                    @pl.when(cond)
                    def _(make=make):
                        make().wait_send()
        swap(step).wait_send()
        return carry

    lax.fori_loop(0, n_blocks, drain, 0)


def fused(amplitudes, integrals, cd_tiles, cd_count):
    n_occ, n_vir = lax.axis_size("occ"), lax.axis_size("vir")
    rows, k = amplitudes.shape
    cd_max = integrals.shape[1]
    side = math.isqrt(rows // n_occ)
    listed, live = cd_tiles[0], cd_count[0]
    slots = jnp.arange(cd_max, dtype=jnp.int32)
    hit = (listed[None, :] == jnp.arange(n_vir, dtype=jnp.int32)[:, None]) & (slots < live)[None, :]
    slot_of = jnp.min(jnp.where(hit, slots[None, :], cd_max), axis=1).astype(jnp.int32)
    block = side * side
    bf16 = jnp.bfloat16
    result = pl.pallas_call(
        functools.partial(ladder_kernel, n_occ, n_vir),
        out_shape=jax.ShapeDtypeStruct((n_occ, block, k), bf16),
        in_specs=[
            pl.BlockSpec(memory_space=pltpu.SMEM),
            pl.BlockSpec(memory_space=pltpu.VMEM),
            pl.BlockSpec(memory_space=pl.ANY),
        ],
        out_specs=pl.BlockSpec(memory_space=pltpu.VMEM),
        scratch_shapes=[
            pltpu.VMEM((n_occ, n_vir, block, k), bf16),
            pltpu.VMEM((cd_max + 1, k, k), bf16),
            pltpu.VMEM((k, k), bf16),
            pltpu.VMEM((block, block), bf16),
            pltpu.VMEM((n_occ, block, k), bf16),
            pltpu.VMEM((n_occ, block, k), bf16),
            pltpu.VMEM((2, block, k), jnp.float32),
            pltpu.VMEM((block, rows), bf16),
            pltpu.SemaphoreType.DMA,
            pltpu.SemaphoreType.DMA((3, 2, n_occ, n_vir)),
            pltpu.SemaphoreType.DMA((2, n_occ, n_vir)),
            pltpu.SemaphoreType.DMA((n_occ,)),
            pltpu.SemaphoreType.DMA((n_occ,)),
        ],
        compiler_params=pltpu.CompilerParams(
            collective_id=0, has_side_effects=True, vmem_limit_bytes=VMEM_BYTES),
        cost_estimate=pl.CostEstimate(
            flops=2 * rows * k * k * (n_vir + 1), bytes_accessed=2 * cd_max * k * k, transcendentals=0),
    )(slot_of, amplitudes, integrals[0])
    return result.reshape(n_occ, side, side, k).transpose(1, 0, 2, 3).reshape(rows, k)


def gathered_whole(amplitudes, integrals, cd_tiles, cd_count):
    n_occ = lax.axis_size("occ")
    rows, k = amplitudes.shape
    side, width = math.isqrt(rows // n_occ), math.isqrt(k)
    listed, live, blocks = cd_tiles[0], cd_count[0], integrals[0]
    gathered = lax.all_gather(amplitudes, "vir", axis=1, tiled=True)

    def visit_slot(slot, running):
        def apply_block(current):
            columns = lax.dynamic_slice_in_dim(gathered, listed[slot] * k, k, 1)
            block = lax.dynamic_index_in_dim(blocks, slot, 0, keepdims=False)
            return current + lax.dot_general(
                columns, block, (((1,), (1,)), ((), ())), preferred_element_type=jnp.float32)

        return lax.cond(slot < live, apply_block, lambda current: current, running)

    zero = jnp.zeros((rows, k), jnp.float32)
    ladder = lax.fori_loop(0, blocks.shape[0], visit_slot, zero).astype(jnp.bfloat16)
    swapped = lax.all_to_all(ladder.reshape(side, n_occ, side, k), "occ", split_axis=1, concat_axis=1, tiled=True)
    swapped = swapped.transpose(2, 1, 0, 3).reshape(rows, k)
    swapped = lax.ppermute(swapped, "vir", [(at, at ^ 1) for at in range(lax.axis_size("vir"))])
    mirrored = swapped.reshape(rows, width, width).transpose(0, 2, 1).reshape(rows, k)
    return (ladder.astype(jnp.float32) + mirrored.astype(jnp.float32)).astype(jnp.bfloat16)


def on_device(amplitudes, integrals, cd_tiles, cd_count):
    rows, k = amplitudes.shape
    needed = 2 * (rows * k * (lax.axis_size("vir") + 6) + (integrals.shape[1] + 2) * k * k)
    run = fused if needed < VMEM_BYTES else gathered_whole
    return run(amplitudes, integrals, cd_tiles, cd_count)


def solution(mesh):
    placed = (P("occ", "vir"), P("vir", None, None, None), P("vir", None), P("vir"))
    return jax.shard_map(
        on_device, mesh=mesh, in_specs=placed, out_specs=P("occ", "vir"), check_vma=False
    )
```
